512 devices in a mesh: dp: 64 (over y, z), tensor: 8 (over x, core).
Axes of the slice: x: 4, y: 4, z: 16, core: 2. Of those that a mesh axis runs over, the one named last changes fastest.
Arguments:
- layer_input: bfloat16 [24576, 4096], P(('dp', 'tensor')), may hold values from -1.5 to 1.5
- value_grad: bfloat16 [24576, 1024], P('dp', 'tensor'), may hold values from -1.1953125 to 1.1953125
- value_weight: bfloat16 [4096, 1024], P(None, 'tensor'), may hold values from -0.375 to 0.375
- error_buffer: bfloat16 [262144, 1024], P('dp', 'tensor'), may hold values from -6 to 6
- query_basis: float32 [1024, 32], P('tensor'), may hold values from -6 to 6
Outputs:
- input_grad: bfloat16 [24576, 4096], P(('dp', 'tensor'))
- error_new: bfloat16 [262144, 1024], P('dp', 'tensor')
- query_new: float32 [1024, 32], P('tensor')
The draws below stay inside these ranges and needn't reach their ends.
All inputs are finite; a program needn't handle non-finite values.
Results may differ from the reference program's by a relative error of at most 0.017.
Values may be sent and summed in bfloat16 or wider, within the bound.
A program may use at most 64 MiB of HBM per device.

```python
import jax
import jax.numpy as jnp
from jax import lax

D = 4096
HD = 128
RANK = 32
TOK_DEV = 384
KV = 1024
TOKENS = 24576
N_DP = 64
N_TENSOR = 8


def levels(rng, dims, cuts, least, high):
    def one(axis_at, parts):
        steps = jax.random.uniform(jax.random.fold_in(jax.random.fold_in(rng, 6), axis_at), (parts,), jnp.float32, least / len(cuts), high / len(cuts))
        return jnp.repeat(jnp.exp(steps), dims[axis_at] // parts).reshape((-1,) + (1,) * (len(dims) - axis_at - 1))

    factor_of = one(*cuts[0])
    for cut in cuts[1:]:
        factor_of = factor_of * one(*cut)
    return factor_of


def normal_values(own_key, shape, spread, limit, cuts=(), held_as=jnp.bfloat16):
    values = jax.random.normal(own_key, shape, jnp.float32) * spread
    if len(cuts) > 0:
        values = levels(own_key, shape, cuts, -0.22, 0.18) * values
    return jnp.clip(values, min=-limit, max=limit).astype(held_as)


def setup_inputs(seed: int = 0) -> dict:
    seeds = jax.random.split(jax.random.key(seed), 6)
    layer_input = normal_values(seeds[0], (TOKENS, D), 0.25, 1.5, ((0, 512),))
    value_grad = normal_values(seeds[1], (TOKENS, KV), 0.2, 1.1953125, ((0, 64), (1, 8)))
    value_weight = normal_values(seeds[2], (D, KV), (2 * HD) ** -0.5, 0.375, ((1, 8),))
    error_buffer = normal_values(seeds[3], (N_DP * D, KV), 1.0, 6.0, ((0, 64), (1, 8)))
    query_basis = normal_values(seeds[4], (KV, RANK), 1.0, 6.0, ((0, 8),), jnp.float32)
    return {"layer_input": layer_input, "value_grad": value_grad, "value_weight": value_weight, "error_buffer": error_buffer, "query_basis": query_basis}


def orthonormal(factor):
    gram_matrix = jnp.dot(factor.T.astype(jnp.float32), factor.astype(jnp.float32), precision=lax.Precision.HIGHEST, preferred_element_type=jnp.float32)
    lower_factor = jnp.linalg.cholesky(gram_matrix)
    return lax.linalg.triangular_solve(lower_factor, factor, left_side=False, lower=True, transpose_a=True)

def reference(layer_input, value_grad, value_weight, error_buffer, query_basis):
    num_heads = N_TENSOR
    inputs_rep = layer_input.reshape(N_DP, TOK_DEV, D)
    grads_rep = value_grad.reshape(N_DP, TOK_DEV, num_heads * HD)
    errors_rep = error_buffer.reshape(N_DP, D, num_heads * HD)

    def replica_moment(triple):
        inputs_one, grads_one, error_one = triple
        product = jnp.dot(inputs_one.T.astype(jnp.float32), grads_one.astype(jnp.float32), preferred_element_type=jnp.float32)
        return product + error_one.astype(jnp.float32)
    moment = lax.map(replica_moment, (inputs_rep, grads_rep, errors_rep))
    moment = moment.reshape(N_DP, D, num_heads, HD)
    basis_in = query_basis.reshape(num_heads, HD, RANK)
    left_sum = jnp.einsum('rdhk,hkq->hdq', moment, basis_in, precision=lax.Precision.HIGHEST) / N_DP
    basis = jax.vmap(orthonormal)(left_sum)
    query_heads = jnp.einsum('rdhk,hdq->hkq', moment, basis, precision=lax.Precision.HIGHEST) / N_DP
    approx = jnp.einsum('hdq,hkq->dhk', basis, query_heads, precision=lax.Precision.HIGHEST)
    error_new = (moment - approx[None]).astype(jnp.bfloat16).reshape(N_DP * D, num_heads * HD)
    total = jnp.zeros((TOKENS, D), jnp.float32)
    for head in range(num_heads):
        term = jnp.dot(value_grad[:, head * HD:(head + 1) * HD].astype(jnp.float32), value_weight[:, head * HD:(head + 1) * HD].T.astype(jnp.float32), preferred_element_type=jnp.float32).astype(jnp.bfloat16)
        term = lax.optimization_barrier(term)
        total = total + term.astype(jnp.float32)
    input_grad = total.astype(jnp.bfloat16)
    return (input_grad, error_new, query_heads.reshape(num_heads * HD, RANK))
```

```python
import functools

import jax
import jax.numpy as jnp
from jax import lax
from jax.experimental import pallas as pl
from jax.experimental.pallas import tpu as pltpu
from jax.sharding import PartitionSpec as P

MESH = pl.DeviceIdType.MESH
F32 = jnp.float32
BF16 = jnp.bfloat16
NY, NZ, NX, NCORE = 4, 16, 4, 2
NT = NX * NCORE
NC = 4


def dot_rows(a, b):
    return lax.dot_general(a, b, (((0,), (0,)), ((), ())), preferred_element_type=F32)


def moment_kernel(
    x_ref, g_ref, e_ref, mom_ref, mean_ref,
    xg, ystage, yrecv, zsum, zstage, zrecv,
    x_send, x_recv, c_send, c_recv, ys_send, ys_recv, zs_send, zs_recv,
    zg_send, zg_recv, yg_send, yg_recv, own_sem,
):
    r, t = lax.axis_index("dp"), lax.axis_index("tensor")
    y, z = r // NZ, lax.rem(r, NZ)
    x, core = t // NCORE, lax.rem(t, NCORE)
    rows, width = x_ref.shape
    ck = width // NC
    py = ck // NY
    pz = py // NZ

    def at_y(d):
        return (lax.rem(y + d, NY) * NZ + z, t)

    def at_z(d):
        return (y * NZ + lax.rem(z + d, NZ), t)

    def at_x(d):
        return (r, lax.rem(x + d, NX) * NCORE + core)

    sibling = (r, x * NCORE + 1 - core)

    barrier = pltpu.get_barrier_semaphore()
    peers = [sibling] + [at_x(d) for d in range(1, NX)] + [at_y(d) for d in range(1, NY)]
    for peer in peers:
        pl.semaphore_signal(barrier, inc=1, device_id=peer, device_id_type=MESH)

    def greet(d, carry):
        pl.semaphore_signal(barrier, inc=1, device_id=at_z(d), device_id_type=MESH)
        return carry

    lax.fori_loop(1, NZ, greet, 0)
    pl.semaphore_wait(barrier, len(peers) + NZ - 1)

    def block(c, owner):
        return xg.at[c, pl.ds(pl.multiple_of(owner * rows, rows), rows)]

    def owner_x(d):
        return lax.rem(x + d, NX) * NCORE + core

    own = []
    sends = []
    for c in range(NC):
        src = x_ref.at[:, pl.ds(c * ck, ck)]
        local = pltpu.make_async_copy(src, block(c, t), own_sem.at[c])
        local.start()
        own.append(local)
        for d in range(1, NX):
            cp = pltpu.make_async_remote_copy(
                src, block(c, t), x_send.at[c, d - 1], x_recv.at[c, d - 1],
                device_id=at_x(d), device_id_type=MESH,
            )
            cp.start()
            sends.append(cp)
        cp = pltpu.make_async_remote_copy(
            src, block(c, t), c_send.at[c, 0], c_recv.at[c, 0],
            device_id=sibling, device_id_type=MESH,
        )
        cp.start()
        sends.append(cp)

    def wait_bytes(ref, sem):
        pltpu.make_async_copy(ref, ref, sem).wait()

    def forward(c):
        for d in range(1, NX):
            got = block(c, owner_x(NX - d))
            wait_bytes(got, x_recv.at[c, d - 1])
            cp = pltpu.make_async_remote_copy(
                got, got, c_send.at[c, d], c_recv.at[c, d],
                device_id=sibling, device_id_type=MESH,
            )
            cp.start()
            sends.append(cp)

    def moment(c):
        own[c].wait()
        for d in range(NX):
            wait_bytes(block(c, t), c_recv.at[c, d])
        def tile(j, carry):
            off = pl.multiple_of(j * py, py)
            at = pl.multiple_of(c * ck + j * py, py)
            m = dot_rows(xg[c, :, pl.ds(off, py)], g_ref[...])
            m = m + e_ref[pl.ds(at, py), :].astype(F32)
            mom_ref[pl.ds(at, py), :] = m
            ystage[c, j] = m.astype(BF16)
            return carry
        lax.fori_loop(0, NY, tile, 0)
        for d in range(1, NY):
            cp = pltpu.make_async_remote_copy(
                ystage.at[c, lax.rem(y + d, NY)], yrecv.at[c, d - 1],
                ys_send.at[c, d - 1], ys_recv.at[c, d - 1],
                device_id=at_y(d), device_id_type=MESH,
            )
            cp.start()
            sends.append(cp)

    def z_scatter(c):
        for d in range(1, NY):
            wait_bytes(yrecv.at[c, d - 1], ys_recv.at[c, d - 1])
        total = mom_ref[pl.ds(pl.multiple_of(c * ck + y * py, py), py), :]
        for d in range(1, NY):
            total = total + yrecv[c, d - 1].astype(F32)
        zsum[c] = total
        zstage[c] = total.astype(BF16)

        def send(d, carry):
            at = pl.multiple_of(lax.rem(z + d, NZ) * pz, pz)
            pltpu.make_async_remote_copy(
                zstage.at[c, pl.ds(at, pz)], zrecv.at[c, d - 1],
                zs_send.at[c], zs_recv.at[c],
                device_id=at_z(d), device_id_type=MESH,
            ).start()
            return carry

        lax.fori_loop(1, NZ, send, 0)

    def z_gather(c):
        wait_bytes(zrecv.at[c], zs_recv.at[c])
        total = zsum[c, pl.ds(pl.multiple_of(z * pz, pz), pz), :]
        for d in range(1, NZ):
            total = total + zrecv[c, d - 1].astype(F32)
        at = pl.multiple_of(c * ck + y * py + z * pz, pz)
        mine = mean_ref.at[pl.ds(at, pz)]
        mine[...] = (total * (1.0 / (NY * NZ))).astype(BF16)

        def send(d, carry):
            pltpu.make_async_remote_copy(
                mine, mine, zg_send.at[c], zg_recv.at[c],
                device_id=at_z(d), device_id_type=MESH,
            ).start()
            return carry

        lax.fori_loop(1, NZ, send, 0)

    def y_gather(c):
        at = pl.multiple_of(c * ck + y * py, py)
        wait_bytes(mean_ref.at[pl.ds(at, py - pz)], zg_recv.at[c])
        mine = mean_ref.at[pl.ds(at, py)]
        for d in range(1, NY):
            cp = pltpu.make_async_remote_copy(
                mine, mine, yg_send.at[c, d - 1], yg_recv.at[c, d - 1],
                device_id=at_y(d), device_id_type=MESH,
            )
            cp.start()
            sends.append(cp)

    def finish(c):
        at = pl.multiple_of(c * ck + y * py, py)
        for d in range(1, NY):
            wait_bytes(mean_ref.at[pl.ds(at, py)], yg_recv.at[c, d - 1])

    stages = [(forward, 0.0), (moment, 1.0), (z_scatter, 6.5), (z_gather, 15.0), (y_gather, 24.0), (finish, 30.0)]
    order = sorted(
        ((4.2 * c + at, i, c, fn) for i, (fn, at) in enumerate(stages) for c in range(NC)),
        key=lambda e: e[:3],
    )
    for _, _, c, fn in order:
        fn(c)

    for cp in sends:
        cp.wait_send()
    for c in range(NC):
        wait_bytes(zrecv.at[c], zs_send.at[c])
        wait_bytes(zrecv.at[c], zg_send.at[c])


def reduce_moment(layer_input, value_grad, error_buffer):
    rows, width = layer_input.shape
    tokens, head = value_grad.shape
    ck = width // NC
    py = ck // NY
    pz = py // NZ
    dma = pltpu.SemaphoreType.DMA
    vmem = pl.BlockSpec(memory_space=pltpu.VMEM)
    return pl.pallas_call(
        moment_kernel,
        out_shape=(
            jax.ShapeDtypeStruct((width, head), F32),
            jax.ShapeDtypeStruct((width, head), BF16),
        ),
        in_specs=[vmem] * 3,
        out_specs=(vmem, vmem),
        scratch_shapes=[
            pltpu.VMEM((NC, tokens, ck), BF16),
            pltpu.VMEM((NC, NY, py, head), BF16),
            pltpu.VMEM((NC, NY - 1, py, head), BF16),
            pltpu.VMEM((NC, py, head), F32),
            pltpu.VMEM((NC, py, head), BF16),
            pltpu.VMEM((NC, NZ - 1, pz, head), BF16),
            dma((NC, NX - 1)), dma((NC, NX - 1)),
            dma((NC, NX)), dma((NC, NX)),
            dma((NC, NY - 1)), dma((NC, NY - 1)),
            dma((NC,)), dma((NC,)),
            dma((NC,)), dma((NC,)),
            dma((NC, NY - 1)), dma((NC, NY - 1)),
            dma((NC,)),
        ],
        compiler_params=pltpu.CompilerParams(
            collective_id=0, has_side_effects=True, vmem_limit_bytes=40 * 2**20
        ),
        name="reduce_moment",
    )(layer_input, value_grad, error_buffer)


def high(a, b):
    return jnp.dot(a, b, precision=lax.Precision.HIGHEST, preferred_element_type=F32)


def finish_kernel(mom_ref, mean_ref, q_ref, err_ref, qn_ref):
    width, head = mean_ref.shape
    rank = q_ref.shape[1]
    tile = 512

    def gram(j, acc):
        m = mean_ref[pl.ds(pl.multiple_of(j * tile, tile), tile), :]
        return acc + dot_rows(m, m)

    k = lax.fori_loop(0, width // tile, gram, jnp.zeros((head, head), F32))
    q = q_ref[...]
    right = high(q.T, k)
    s = high(right, q)
    row_of = lax.broadcasted_iota(jnp.int32, (rank, 1), 0)
    out = jnp.zeros((rank, head), F32)
    for i in range(rank):
        pivot = s[i:i + 1, i:i + 1]
        inv = 1.0 / pivot
        srow = s[i:i + 1, :] * inv
        rrow = right[i:i + 1, :] * inv
        mine = row_of == i
        out = jnp.where(mine, rrow * jnp.sqrt(pivot), out)
        col = jnp.where(mine, 0.0, s[:, i:i + 1])
        s = jnp.where(mine, srow, s - col * srow)
        right = jnp.where(mine, rrow, right - col * rrow)
    qn_ref[...] = out.T
    b = high(q, right)
    b_hi = b.astype(BF16)
    b_lo = (b - b_hi.astype(F32)).astype(BF16)

    def error(j, carry):
        at = pl.ds(pl.multiple_of(j * tile, tile), tile)
        m = mean_ref[at, :]
        approx = jnp.dot(m, b_hi, preferred_element_type=F32) + jnp.dot(m, b_lo, preferred_element_type=F32)
        err_ref[at, :] = (mom_ref[at, :] - approx).astype(BF16)
        return carry

    lax.fori_loop(0, width // tile, error, 0)


def finish(mom, mean, query_basis):
    vmem = pl.BlockSpec(memory_space=pltpu.VMEM)
    return pl.pallas_call(
        finish_kernel,
        out_shape=(
            jax.ShapeDtypeStruct(mean.shape, BF16),
            jax.ShapeDtypeStruct(query_basis.shape, F32),
        ),
        in_specs=[vmem] * 3,
        out_specs=(vmem, vmem),
        compiler_params=pltpu.CompilerParams(vmem_limit_bytes=32 * 2**20),
        name="finish",
    )(mom, mean, query_basis)


def per_device(layer_input, value_grad, value_weight, error_buffer, query_basis):
    term = lax.dot_general(
        value_grad, value_weight, (((1,), (1,)), ((), ())), preferred_element_type=F32
    ).astype(BF16)
    summed = lax.psum_scatter(term, "tensor", scatter_dimension=0, tiled=True)
    mom, mean = reduce_moment(layer_input, value_grad, error_buffer)
    error_new, query_new = finish(mom, mean, query_basis)
    return (summed, error_new, query_new)


def solution(mesh):
    return jax.shard_map(
        per_device,
        mesh=mesh,
        in_specs=(
            P(("dp", "tensor"), None),
            P("dp", "tensor"),
            P(None, "tensor"),
            P("dp", "tensor"),
            P("tensor", None),
        ),
        out_specs=(P(("dp", "tensor"), None), P("dp", "tensor"), P("tensor", None)),
        check_vma=False,
    )
```

```python
import functools

import jax
import jax.numpy as jnp
from jax import lax
from jax.experimental import pallas as pl
from jax.experimental.pallas import tpu as pltpu
from jax.sharding import PartitionSpec as P

MESH = pl.DeviceIdType.MESH
F32 = jnp.float32
BF16 = jnp.bfloat16
NY, NZ, NX, NCORE = 4, 16, 4, 2
NT = NX * NCORE
NC = 4
AHEAD = 2
FAR_FIRST = sorted(range(1, NZ), key=lambda d: -min(d, NZ - d))


def dot_rows(a, b):
    return lax.dot_general(a, b, (((0,), (0,)), ((), ())), preferred_element_type=F32)


def high(a, b, dims):
    return lax.dot_general(
        a, b, (dims, ((), ())), precision=lax.Precision.HIGHEST, preferred_element_type=F32
    )


def kernel(
    x_hbm, g_hbm, w_hbm, e_hbm, q_ref,
    ig_hbm, err_hbm, qn_ref,
    g_ref, w_ref, e_ref,
    xg, mom_ref, mean_ref, ystage, yrecv, zsum, zstage, zrecv, gram_ref,
    term, other, pair, pair_recv, home, ig_ref, err_ref,
    out_sem, load_sem, entered,
    x_send, x_recv, c_send, c_recv, ys_send, ys_recv, zs_send, zs_recv,
    zg_send, zg_recv, yg_send, yg_recv, t_send, t_recv, p_send, p_recv, own_sem,
):
    r, t = lax.axis_index("dp"), lax.axis_index("tensor")
    y, z = r // NZ, lax.rem(r, NZ)
    x, core = t // NCORE, lax.rem(t, NCORE)
    rows, width = x_hbm.shape
    tokens, head = g_hbm.shape
    rank = q_ref.shape[0]
    ck = width // NC
    py = ck // NY
    pz = py // NZ
    wide = 512

    def at_y(d):
        return (lax.rem(y + d, NY) * NZ + z, t)

    def at_z(d):
        return (y * NZ + lax.rem(z + d, NZ), t)

    def owner_x(d, c):
        return lax.rem(x + d, NX) * NCORE + c

    def at_x(d):
        return (r, owner_x(d, core))

    sibling = (r, x * NCORE + 1 - core)

    barrier = pltpu.get_barrier_semaphore()
    peers = [at_x(1), at_x(3), sibling, at_x(2), at_z(1), at_z(NZ - 1), at_y(1), at_y(3), at_y(2)]
    for peer in peers:
        pl.semaphore_signal(barrier, inc=1, device_id=peer, device_id_type=MESH)

    loads = [
        pltpu.make_async_copy(src, dst, load_sem.at[i])
        for i, (src, dst) in enumerate(((g_hbm, g_ref), (w_hbm, w_ref), (e_hbm, e_ref)))
    ]
    for cp in loads:
        cp.start()

    def block(c, owner, part=slice(None)):
        return xg.at[c, pl.ds(pl.multiple_of(owner * rows, rows), rows), part]

    own = []
    for c in range(NC):
        own.append(pltpu.make_async_copy(x_hbm.at[:, pl.ds(c * ck, ck)], block(c, t), own_sem.at[c]))
        own[c].start()
    pl.semaphore_wait(barrier, len(peers))

    sends = []

    def remote(src, dst, send, recv, device):
        cp = pltpu.make_async_remote_copy(
            src, dst, send, recv, device_id=device, device_id_type=MESH
        )
        cp.start()
        sends.append(cp)

    def spread(c):
        src = x_hbm.at[:, pl.ds(c * ck, ck)]
        remote(src, block(c, t), x_send.at[c, 0], x_recv.at[c, 0], at_x(1))
        remote(src, block(c, t), x_send.at[c, 1], x_recv.at[c, 1], at_x(3))
        remote(src, block(c, t), c_send.at[c, 0], c_recv.at[c, 0], sibling)

    def greet(i):
        if i > 0:
            pl.semaphore_wait(entered.at[i - 1], 2)
        if i < 3:
            for d in (2**i, NZ - 2**i):
                pl.semaphore_signal(entered.at[i], inc=1, device_id=at_z(d), device_id_type=MESH)

    def row_block(ref, owner):
        return ref.at[pl.ds(pl.multiple_of(owner * rows, rows), rows)]

    def head_term(c):
        if c == 0:
            loads[1].wait()

        def tile(j, carry):
            at = pl.ds(pl.multiple_of(j * wide, wide), wide)
            term[:, at] = lax.dot_general(
                g_ref[...], w_ref[at, :], (((1,), (1,)), ((), ())), preferred_element_type=F32
            ).astype(BF16)
            return carry

        half = width // wide // 2
        lax.fori_loop(c * half, (c + 1) * half, tile, 0)
        if c == 0:
            return
        for d in range(NX):
            remote(
                row_block(term, owner_x(d, 1 - core)), other.at[d],
                t_send.at[d], t_recv.at[d], sibling,
            )

    def wait_bytes(ref, sem):
        pltpu.make_async_copy(ref, ref, sem).wait()

    left, right = pl.ds(0, ck // 2), pl.ds(ck // 2, ck // 2)

    def forward(c):
        for i, (d, part, to) in enumerate(((3, left, 1), (1, right, 3))):
            owner = owner_x(d, core)
            got = block(c, owner)
            wait_bytes(got, x_recv.at[c, i])
            half = block(c, owner, part)
            remote(half, half, x_send.at[c, 2 + i], x_recv.at[c, 2 + i], at_x(to))
            remote(got, got, c_send.at[c, 1 + i], c_recv.at[c, 1 + i], sibling)
        if c + AHEAD < NC:
            spread(c + AHEAD)

    def forward_far(c):
        owner = owner_x(2, core)
        wait_bytes(block(c, owner, left), x_recv.at[c, 2])
        wait_bytes(block(c, owner, right), x_recv.at[c, 3])
        got = block(c, owner)
        remote(got, got, c_send.at[c, 3], c_recv.at[c, 3], sibling)

    def moment(c):
        own[c].wait()
        if c == 0:
            loads[0].wait()
            loads[2].wait()
        for d in range(NX):
            wait_bytes(block(c, t), c_recv.at[c, d])

        def tile(j, carry):
            off = pl.multiple_of(j * py, py)
            at = pl.multiple_of(c * ck + j * py, py)
            m = dot_rows(xg[c, :, pl.ds(off, py)], g_ref[...])
            m = m + e_ref[pl.ds(at, py), :].astype(F32)
            mom_ref[pl.ds(at, py), :] = m
            ystage[c, j] = m.astype(BF16)
            return carry

        lax.fori_loop(0, NY, tile, 0)
        for d in (1, 3, 2):
            remote(
                ystage.at[c, lax.rem(y + d, NY)], yrecv.at[c, d - 1],
                ys_send.at[c, d - 1], ys_recv.at[c, d - 1], at_y(d),
            )

    def z_scatter(c):
        for d in range(1, NY):
            wait_bytes(yrecv.at[c, d - 1], ys_recv.at[c, d - 1])
        total = mom_ref[pl.ds(pl.multiple_of(c * ck + y * py, py), py), :]
        for d in range(1, NY):
            total = total + yrecv[c, d - 1].astype(F32)
        zsum[c] = total
        zstage[c] = total.astype(BF16)

        for d in FAR_FIRST:
            at = pl.multiple_of(lax.rem(z + d, NZ) * pz, pz)
            pltpu.make_async_remote_copy(
                zstage.at[c, pl.ds(at, pz)], zrecv.at[c, d - 1],
                zs_send.at[c], zs_recv.at[c],
                device_id=at_z(d), device_id_type=MESH,
            ).start()

    def z_gather(c):
        wait_bytes(zrecv.at[c], zs_recv.at[c])
        total = zsum[c, pl.ds(pl.multiple_of(z * pz, pz), pz), :]
        for d in range(1, NZ):
            total = total + zrecv[c, d - 1].astype(F32)
        at = pl.multiple_of(c * ck + y * py + z * pz, pz)
        mine = mean_ref.at[pl.ds(at, pz)]
        mine[...] = (total * (1.0 / (NY * NZ))).astype(BF16)

        for d in FAR_FIRST:
            pltpu.make_async_remote_copy(
                mine, mine, zg_send.at[c], zg_recv.at[c],
                device_id=at_z(d), device_id_type=MESH,
            ).start()

    def y_gather(c):
        at = pl.multiple_of(c * ck + y * py, py)
        wait_bytes(mean_ref.at[pl.ds(at, py - pz)], zg_recv.at[c])
        mine = mean_ref.at[pl.ds(at, py)]
        for d in (1, 3, 2):
            remote(mine, mine, yg_send.at[c, d - 1], yg_recv.at[c, d - 1], at_y(d))

    def gram(c):
        at = pl.multiple_of(c * ck + y * py, py)
        for d in range(1, NY):
            wait_bytes(mean_ref.at[pl.ds(at, py)], yg_recv.at[c, d - 1])
        m = mean_ref[pl.ds(c * ck, ck), :]
        part = dot_rows(m, m)
        gram_ref[...] = part if c == 0 else gram_ref[...] + part

    def pair_sum(c):
        for d in range(NX):
            wait_bytes(other.at[d], t_recv.at[d])
        for d in range(NX):
            mine = row_block(term, owner_x(d, core))

            def tile(j, carry):
                at = pl.ds(pl.multiple_of(j * wide, wide), wide)
                both = mine[:, at].astype(F32) + other[d, :, at].astype(F32)
                if d == 0:
                    home[:, at] = both
                else:
                    pair[d - 1, :, at] = both.astype(BF16)
                return carry

            lax.fori_loop(0, width // wide, tile, 0)

    def pair_send(c):
        for d in (1, 3, 2):
            remote(pair.at[d - 1], pair_recv.at[d - 1], p_send.at[d - 1], p_recv.at[d - 1], at_x(d))

    stores = []

    def store(src, dst):
        cp = pltpu.make_async_copy(src, dst, out_sem.at[len(stores)])
        cp.start()
        stores.append(cp)

    def input_grad(c):
        for d in range(1, NX):
            wait_bytes(pair_recv.at[d - 1], p_recv.at[d - 1])

        def tile(j, carry):
            at = pl.ds(pl.multiple_of(j * wide, wide), wide)
            total = home[:, at]
            for d in range(1, NX):
                total = total + pair_recv[d - 1, :, at].astype(F32)
            ig_ref[:, at] = total.astype(BF16)
            return carry

        lax.fori_loop(0, width // wide, tile, 0)
        store(ig_ref, ig_hbm)

    stages = [
        (forward, 4.5), (forward_far, 8.7), (moment, 9.7), (z_scatter, 15.2), (z_gather, 24.0),
        (y_gather, 33.5), (gram, 39.0),
    ]
    order = [(2.6 * c + at, i, c, fn) for i, (fn, at) in enumerate(stages) for c in range(NC)]
    order += [
        (0.0, 0, 0, greet), (18.0, 0, 0, head_term), (3.0, 0, 1, greet), (18.5, 0, 1, head_term),
        (6.0, 0, 2, greet), (13.0, 0, 3, greet),
        (21.0, 9, 0, pair_sum), (21.1, 9, 0, pair_send), (40.0, 9, 0, input_grad),
    ]
    for c in range(AHEAD):
        spread(c)
    for _, _, c, fn in sorted(order, key=lambda e: e[:3]):
        fn(c)

    q = q_ref[...]
    prod = high(q, gram_ref[...], ((1,), (0,)))
    s = high(prod, q, ((1,), (1,)))
    row_of = lax.broadcasted_iota(jnp.int32, (rank, 1), 0)
    out = jnp.zeros((rank, head), F32)
    for i in range(rank):
        pivot = s[i:i + 1, i:i + 1]
        inv = 1.0 / pivot
        srow = s[i:i + 1, :] * inv
        rrow = prod[i:i + 1, :] * inv
        mine = row_of == i
        out = jnp.where(mine, rrow * jnp.sqrt(pivot), out)
        col = jnp.where(mine, 0.0, s[:, i:i + 1])
        s = jnp.where(mine, srow, s - col * srow)
        prod = jnp.where(mine, rrow, prod - col * rrow)
    qn_ref[...] = out
    b = high(q, prod, ((0,), (0,)))
    b_hi = b.astype(BF16)
    b_both = jnp.concatenate([b_hi, (b - b_hi.astype(F32)).astype(BF16)], axis=0)

    for j in range(width // wide):
        at = pl.ds(j * wide, wide)
        m = mean_ref[at, :]
        approx = jnp.dot(jnp.concatenate([m, m], axis=1), b_both, preferred_element_type=F32)
        err_ref[at, :] = (mom_ref[at, :] - approx).astype(BF16)
        store(err_ref.at[at], err_hbm.at[at])

    for cp in stores:
        cp.wait()
    for cp in sends:
        cp.wait_send()
    for c in range(NC):
        wait_bytes(zrecv.at[c], zs_send.at[c])
        wait_bytes(zrecv.at[c], zg_send.at[c])


def deliver_kernel(*refs):
    n = len(refs) // 2
    for src, dst in zip(refs[:n], refs[n:]):
        dst[...] = src[...]


def deliver(*arrays):
    vmem = pl.BlockSpec(memory_space=pltpu.VMEM)
    return pl.pallas_call(
        deliver_kernel,
        out_shape=tuple(jax.ShapeDtypeStruct(a.shape, a.dtype) for a in arrays),
        in_specs=[vmem] * len(arrays),
        out_specs=(vmem,) * len(arrays),
        compiler_params=pltpu.CompilerParams(vmem_limit_bytes=56 * 2**20),
        name="deliver",
    )(*arrays)


def per_device(layer_input, value_grad, value_weight, error_buffer, query_basis):
    rows, width = layer_input.shape
    tokens, head = value_grad.shape
    rank = query_basis.shape[1]
    ck = width // NC
    py = ck // NY
    pz = py // NZ
    dma = pltpu.SemaphoreType.DMA
    vmem = pl.BlockSpec(memory_space=pltpu.VMEM)
    hbm = pl.BlockSpec(memory_space=pltpu.HBM)
    input_grad, error_new, query_new = pl.pallas_call(
        kernel,
        out_shape=(
            jax.ShapeDtypeStruct((rows, width), BF16),
            jax.ShapeDtypeStruct((width, head), BF16),
            jax.ShapeDtypeStruct((rank, head), F32),
        ),
        in_specs=[hbm] * 4 + [vmem],
        out_specs=(hbm, hbm, vmem),
        scratch_shapes=[
            pltpu.VMEM((tokens, head), BF16),
            pltpu.VMEM((width, head), BF16),
            pltpu.VMEM((width, head), BF16),
            pltpu.VMEM((NC, tokens, ck), BF16),
            pltpu.VMEM((width, head), F32),
            pltpu.VMEM((width, head), BF16),
            pltpu.VMEM((NC, NY, py, head), BF16),
            pltpu.VMEM((NC, NY - 1, py, head), BF16),
            pltpu.VMEM((NC, py, head), F32),
            pltpu.VMEM((NC, py, head), BF16),
            pltpu.VMEM((NC, NZ - 1, pz, head), BF16),
            pltpu.VMEM((head, head), F32),
            pltpu.VMEM((tokens, width), BF16),
            pltpu.VMEM((NX, rows, width), BF16),
            pltpu.VMEM((NX - 1, rows, width), BF16),
            pltpu.VMEM((NX - 1, rows, width), BF16),
            pltpu.VMEM((rows, width), F32),
            pltpu.VMEM((rows, width), BF16),
            pltpu.VMEM((width, head), BF16),
            dma((1 + width // 512,)),
            dma((3,)), pltpu.SemaphoreType.REGULAR((3,)),
            dma((NC, 4)), dma((NC, 4)),
            dma((NC, NX)), dma((NC, NX)),
            dma((NC, NY - 1)), dma((NC, NY - 1)),
            dma((NC,)), dma((NC,)),
            dma((NC,)), dma((NC,)),
            dma((NC, NY - 1)), dma((NC, NY - 1)),
            dma((NX,)), dma((NX,)),
            dma((NX - 1,)), dma((NX - 1,)),
            dma((NC,)),
        ],
        compiler_params=pltpu.CompilerParams(
            collective_id=0, has_side_effects=True, vmem_limit_bytes=56 * 2**20
        ),
        name="value_backward",
    )(layer_input, value_grad, value_weight, error_buffer, query_basis.T)
    input_grad, error_new, query_new = deliver(input_grad, error_new, query_new)
    return (input_grad, error_new, query_new.T)


def solution(mesh):
    return jax.shard_map(
        per_device,
        mesh=mesh,
        in_specs=(
            P(("dp", "tensor"), None),
            P("dp", "tensor"),
            P(None, "tensor"),
            P("dp", "tensor"),
            P("tensor", None),
        ),
        out_specs=(P(("dp", "tensor"), None), P("dp", "tensor"), P("tensor", None)),
        check_vma=False,
    )
```

```python
import functools

import jax
import jax.numpy as jnp
from jax import lax
from jax.experimental import pallas as pl
from jax.experimental.pallas import tpu as pltpu
from jax.sharding import PartitionSpec as P

MESH = pl.DeviceIdType.MESH
F32 = jnp.float32
BF16 = jnp.bfloat16
NY, NZ, NX, NCORE = 4, 16, 4, 2
NT = NX * NCORE
NC = 4
AHEAD = 2
FAR_FIRST = sorted(range(1, NZ), key=lambda d: -min(d, NZ - d))


def dot_rows(a, b):
    return lax.dot_general(a, b, (((0,), (0,)), ((), ())), preferred_element_type=F32)


def high(a, b, dims):
    return lax.dot_general(
        a, b, (dims, ((), ())), precision=lax.Precision.HIGHEST, preferred_element_type=F32
    )


def kernel(
    x_hbm, g_hbm, w_hbm, e_hbm, q_ref,
    ig_hbm, err_hbm, qn_ref,
    g_ref, w_ref, e_ref,
    xg, mom_ref, mean_ref, ystage, yrecv, zsum, zstage, zrecv, gram_ref,
    term, other, pair, pair_recv, home, ig_ref, err_ref,
    out_sem, load_sem, entered,
    x_send, x_recv, c_send, c_recv, ys_send, ys_recv, zs_send, zs_recv,
    zg_send, zg_recv, yg_send, yg_recv, t_send, t_recv, p_send, p_recv, own_sem,
):
    r, t = lax.axis_index("dp"), lax.axis_index("tensor")
    y, z = r // NZ, lax.rem(r, NZ)
    x, core = t // NCORE, lax.rem(t, NCORE)
    rows, width = x_hbm.shape
    tokens, head = g_hbm.shape
    rank = q_ref.shape[0]
    ck = width // NC
    py = ck // NY
    pz = py // NZ
    wide = 512

    def at_y(d):
        return (lax.rem(y + d, NY) * NZ + z, t)

    def at_z(d):
        return (y * NZ + lax.rem(z + d, NZ), t)

    def owner_x(d, c):
        return lax.rem(x + d, NX) * NCORE + c

    def at_x(d):
        return (r, owner_x(d, core))

    sibling = (r, x * NCORE + 1 - core)

    barrier = pltpu.get_barrier_semaphore()
    peers = [at_x(1), at_x(3), sibling, at_x(2), at_z(1), at_z(NZ - 1), at_y(1), at_y(3), at_y(2)]
    for peer in peers:
        pl.semaphore_signal(barrier, inc=1, device_id=peer, device_id_type=MESH)

    loads = [
        pltpu.make_async_copy(src, dst, load_sem.at[i])
        for i, (src, dst) in enumerate(((g_hbm, g_ref), (w_hbm, w_ref), (e_hbm, e_ref)))
    ]
    for cp in loads:
        cp.start()

    def block(c, owner, part=slice(None)):
        return xg.at[c, pl.ds(pl.multiple_of(owner * rows, rows), rows), part]

    own = []
    for c in range(NC):
        own.append(pltpu.make_async_copy(x_hbm.at[:, pl.ds(c * ck, ck)], block(c, t), own_sem.at[c]))
        own[c].start()
    pl.semaphore_wait(barrier, len(peers))

    sends = []

    def remote(src, dst, send, recv, device):
        cp = pltpu.make_async_remote_copy(
            src, dst, send, recv, device_id=device, device_id_type=MESH
        )
        cp.start()
        sends.append(cp)

    def spread(c):
        src = x_hbm.at[:, pl.ds(c * ck, ck)]
        remote(src, block(c, t), x_send.at[c, 0], x_recv.at[c, 0], at_x(1))
        remote(src, block(c, t), x_send.at[c, 1], x_recv.at[c, 1], at_x(3))
        remote(src, block(c, t), c_send.at[c, 0], c_recv.at[c, 0], sibling)

    def greet(i):
        if i > 0:
            pl.semaphore_wait(entered.at[i - 1], 2)
        if i < 3:
            for d in (2**i, NZ - 2**i):
                pl.semaphore_signal(entered.at[i], inc=1, device_id=at_z(d), device_id_type=MESH)

    def row_block(ref, owner):
        return ref.at[pl.ds(pl.multiple_of(owner * rows, rows), rows)]

    def head_term(i):
        if i == 0:
            loads[1].wait()

        def tile(j, carry):
            at = pl.ds(pl.multiple_of(j * wide, wide), wide)
            term[:, at] = lax.dot_general(
                g_ref[...], w_ref[at, :], (((1,), (1,)), ((), ())), preferred_element_type=F32
            ).astype(BF16)
            return carry

        quarter = width // wide // 4
        lax.fori_loop(i * quarter, (i + 1) * quarter, tile, 0)

    def term_send(i):
        for d in (1, 3, 2, 0):
            remote(
                row_block(term, owner_x(d, 1 - core)), other.at[d],
                t_send.at[d], t_recv.at[d], sibling,
            )

    def wait_bytes(ref, sem):
        pltpu.make_async_copy(ref, ref, sem).wait()

    left, right = pl.ds(0, ck // 2), pl.ds(ck // 2, ck // 2)

    def forward(c):
        for i, (d, part, to) in enumerate(((3, left, 1), (1, right, 3))):
            owner = owner_x(d, core)
            got = block(c, owner)
            wait_bytes(got, x_recv.at[c, i])
            half = block(c, owner, part)
            remote(half, half, x_send.at[c, 2 + i], x_recv.at[c, 2 + i], at_x(to))
            remote(got, got, c_send.at[c, 1 + i], c_recv.at[c, 1 + i], sibling)
        if c + AHEAD < NC:
            spread(c + AHEAD)

    def forward_far(c):
        owner = owner_x(2, core)
        wait_bytes(block(c, owner, left), x_recv.at[c, 2])
        wait_bytes(block(c, owner, right), x_recv.at[c, 3])
        got = block(c, owner)
        remote(got, got, c_send.at[c, 3], c_recv.at[c, 3], sibling)

    def moment(c):
        own[c].wait()
        if c == 0:
            loads[0].wait()
            loads[2].wait()
        for d in range(NX):
            wait_bytes(block(c, t), c_recv.at[c, d])

        for d in (1, 3, 2, 0):
            j = lax.rem(y + d, NY)
            off = pl.multiple_of(j * py, py)
            at = pl.multiple_of(c * ck + j * py, py)
            m = dot_rows(xg[c, :, pl.ds(off, py)], g_ref[...])
            m = m + e_ref[pl.ds(at, py), :].astype(F32)
            mom_ref[pl.ds(at, py), :] = m
            if d > 0:
                ystage[c, d - 1] = m.astype(BF16)
                remote(
                    ystage.at[c, d - 1], yrecv.at[c, d - 1],
                    ys_send.at[c, d - 1], ys_recv.at[c, d - 1], at_y(d),
                )

    def z_scatter(c):
        for d in range(1, NY):
            wait_bytes(yrecv.at[c, d - 1], ys_recv.at[c, d - 1])
        total = mom_ref[pl.ds(pl.multiple_of(c * ck + y * py, py), py), :]
        for d in range(1, NY):
            total = total + yrecv[c, d - 1].astype(F32)
        zsum[c] = total
        zstage[c] = total.astype(BF16)

        for d in FAR_FIRST:
            at = pl.multiple_of(lax.rem(z + d, NZ) * pz, pz)
            pltpu.make_async_remote_copy(
                zstage.at[c, pl.ds(at, pz)], zrecv.at[c, d - 1],
                zs_send.at[c], zs_recv.at[c],
                device_id=at_z(d), device_id_type=MESH,
            ).start()

    group = NZ // 4

    def z_gather(c):
        wait_bytes(zrecv.at[c], zs_recv.at[c])
        total = zsum[c, pl.ds(pl.multiple_of(z * pz, pz), pz), :]
        for d in range(1, NZ):
            total = total + zrecv[c, d - 1].astype(F32)
        at = pl.multiple_of(c * ck + y * py + z * pz, pz)
        mine = mean_ref.at[pl.ds(at, pz)]
        mine[...] = (total * (1.0 / (NY * NZ))).astype(BF16)
        for d in FAR_FIRST:
            ahead = lax.rem(z // group + 4 - lax.rem(z + d, NZ) // group, 4)
            pltpu.make_async_remote_copy(
                mine, mine, zg_send.at[c], zg_recv.at[c, ahead],
                device_id=at_z(d), device_id_type=MESH,
            ).start()

    def y_gather(c):
        for d in (0, 1, 3, 2):
            owner = lax.rem(z // group + d, 4)
            at = pl.multiple_of(c * ck + y * py + owner * group * pz, pz)
            come = group * pz - (pz if d == 0 else 0)
            wait_bytes(mean_ref.at[pl.ds(at, come)], zg_recv.at[c, d])
            mine = mean_ref.at[pl.ds(at, group * pz)]
            for dy in (2, 1, 3):
                pltpu.make_async_remote_copy(
                    mine, mine, yg_send.at[c], yg_recv.at[c],
                    device_id=at_y(dy), device_id_type=MESH,
                ).start()

    def gram(c):
        def add(rows_at, first):
            m = mean_ref[rows_at, :]
            part = dot_rows(m, m)
            gram_ref[...] = part if first else gram_ref[...] + part

        wait_bytes(mean_ref.at[pl.ds(0, (NY - 1) * py)], yg_recv.at[c])
        add(pl.ds(c * ck, ck), c == 0)

    def pair_sum(d):
        wait_bytes(other.at[d], t_recv.at[d])
        mine = row_block(term, owner_x(d, core))

        def tile(j, carry):
            at = pl.ds(pl.multiple_of(j * wide, wide), wide)
            both = mine[:, at].astype(F32) + other[d, :, at].astype(F32)
            if d == 0:
                home[:, at] = both
            else:
                pair[d - 1, :, at] = both.astype(BF16)
            return carry

        lax.fori_loop(0, width // wide, tile, 0)
        if d > 0:
            remote(pair.at[d - 1], pair_recv.at[d - 1], p_send.at[d - 1], p_recv.at[d - 1], at_x(d))

    stores = []

    def store(src, dst):
        cp = pltpu.make_async_copy(src, dst, out_sem.at[len(stores)])
        cp.start()
        stores.append(cp)

    def input_grad(c):
        for d in range(1, NX):
            wait_bytes(pair_recv.at[d - 1], p_recv.at[d - 1])

        def tile(j, carry):
            at = pl.ds(pl.multiple_of(j * wide, wide), wide)
            total = home[:, at]
            for d in range(1, NX):
                total = total + pair_recv[d - 1, :, at].astype(F32)
            ig_ref[:, at] = total.astype(BF16)
            return carry

        lax.fori_loop(0, width // wide, tile, 0)
        store(ig_ref, ig_hbm)

    def drain(c):
        while sends:
            sends.pop().wait_send()

    def drain_z(c):
        for c in range(NC):
            wait_bytes(zrecv.at[c], zs_send.at[c])

    stages = [
        (forward, 4.5), (forward_far, 8.7), (moment, 9.7), (z_scatter, 15.2), (z_gather, 24.0),
        (y_gather, 33.5), (gram, 39.0),
    ]
    order = [(2.6 * c + at, i, c, fn) for i, (fn, at) in enumerate(stages) for c in range(NC)]
    order += [
        (0.0, 0, 0, greet), (3.0, 0, 1, greet), (6.0, 0, 2, greet), (13.0, 0, 3, greet),
        (16.0, 9, 0, head_term), (18.6, 9, 1, head_term), (21.2, 9, 2, head_term), (23.1, 9, 3, head_term),
        (23.2, 9, 0, term_send), (26.7, 9, 1, pair_sum), (29.3, 9, 3, pair_sum), (31.9, 9, 2, pair_sum),
        (34.5, 9, 0, pair_sum), (47.0, 9, 0, input_grad), (46.0, 9, 0, drain_z),
        (46.1, 9, 0, drain),
    ]
    for c in range(AHEAD):
        spread(c)
    for _, _, c, fn in sorted(order, key=lambda e: e[:3]):
        fn(c)

    q = q_ref[...]
    prod = high(q, gram_ref[...], ((1,), (0,)))
    unit = lax.rsqrt(jnp.sum(prod * q, axis=1, keepdims=True))
    q, prod = q * unit, prod * unit
    s = high(prod, jnp.concatenate([q, jnp.zeros((head - rank, head), F32)], axis=0), ((1,), (1,)))
    row_of = lax.broadcasted_iota(jnp.int32, (rank, head), 0)
    out = jnp.zeros((rank, head), F32)
    for i in range(0, rank, 2):
        col0 = jnp.broadcast_to(s[:, i:i + 1], (rank, head))
        col1 = jnp.broadcast_to(s[:, i + 1:i + 2], (rank, head))
        a, b, d = col0[i:i + 1, :], col1[i:i + 1, :], col1[i + 1:i + 2, :]
        det = a * d - b * b
        inv = 1.0 / det
        s0, s1 = s[i:i + 1, :], s[i + 1:i + 2, :]
        p0, p1 = prod[i:i + 1, :], prod[i + 1:i + 2, :]
        first, second = row_of == i, row_of == i + 1
        out = jnp.where(first, p0 * lax.rsqrt(a), out)
        out = jnp.where(second, (p1 - (b / a) * p0) * lax.rsqrt(det / a), out)
        n0, n1 = (d * s0 - b * s1) * inv, (a * s1 - b * s0) * inv
        s = jnp.where(first, n0, jnp.where(second, n1, s - col0 * n0 - col1 * n1))
        n0, n1 = (d * p0 - b * p1) * inv, (a * p1 - b * p0) * inv
        prod = jnp.where(first, n0, jnp.where(second, n1, prod - col0 * n0 - col1 * n1))
    qn_ref[...] = out
    b = high(q, prod, ((0,), (0,)))
    b_hi = b.astype(BF16)
    b_both = jnp.concatenate([b_hi, (b - b_hi.astype(F32)).astype(BF16)], axis=0)

    for j in range(width // wide):
        at = pl.ds(j * wide, wide)
        m = mean_ref[at, :]
        approx = jnp.dot(jnp.concatenate([m, m], axis=1), b_both, preferred_element_type=F32)
        err_ref[at, :] = (mom_ref[at, :] - approx).astype(BF16)
        store(err_ref.at[at], err_hbm.at[at])

    for cp in stores:
        cp.wait()
    drain(0)
    for c in range(NC):
        wait_bytes(zrecv.at[c], zg_send.at[c])
        wait_bytes(mean_ref.at[pl.ds(0, (NY - 1) * py)], yg_send.at[c])


def deliver_kernel(
    ig_in, err_in, qn_in, ig_out, err_out, qn_out, ig_ref, err_ref, qn_ref, load_sem, store_sem
):
    n = load_sem.shape[0] - 2
    tile = err_in.shape[0] // n
    parts = [
        (err_in.at[at], err_ref.at[at], err_out.at[at])
        for at in (pl.ds(j * tile, tile) for j in range(n))
    ] + [(ig_in, ig_ref, ig_out), (qn_in, qn_ref, qn_out)]
    loads = [pltpu.make_async_copy(a, b, load_sem.at[i]) for i, (a, b, _) in enumerate(parts)]
    stores = [pltpu.make_async_copy(b, c, store_sem.at[i]) for i, (_, b, c) in enumerate(parts)]
    for cp in loads:
        cp.start()
    for load, out in zip(loads, stores):
        load.wait()
        out.start()
    for cp in stores:
        cp.wait()


def deliver(*arrays):
    hbm = pl.BlockSpec(memory_space=pl.ANY)
    n = 4
    return pl.pallas_call(
        deliver_kernel,
        out_shape=tuple(jax.ShapeDtypeStruct(a.shape, a.dtype) for a in arrays),
        in_specs=[hbm] * len(arrays),
        out_specs=(hbm,) * len(arrays),
        scratch_shapes=[pltpu.VMEM(a.shape, a.dtype) for a in arrays]
        + [pltpu.SemaphoreType.DMA((n + 2,))] * 2,
        compiler_params=pltpu.CompilerParams(vmem_limit_bytes=56 * 2**20),
        name="deliver",
    )(*arrays)


def per_device(layer_input, value_grad, value_weight, error_buffer, query_basis):
    rows, width = layer_input.shape
    tokens, head = value_grad.shape
    rank = query_basis.shape[1]
    ck = width // NC
    py = ck // NY
    pz = py // NZ
    dma = pltpu.SemaphoreType.DMA
    vmem = pl.BlockSpec(memory_space=pltpu.VMEM)
    hbm = pl.BlockSpec(memory_space=pltpu.HBM)
    input_grad, error_new, query_new = pl.pallas_call(
        kernel,
        out_shape=(
            jax.ShapeDtypeStruct((rows, width), BF16),
            jax.ShapeDtypeStruct((width, head), BF16),
            jax.ShapeDtypeStruct((rank, head), F32),
        ),
        in_specs=[hbm] * 4 + [vmem],
        out_specs=(hbm, hbm, vmem),
        scratch_shapes=[
            pltpu.VMEM((tokens, head), BF16),
            pltpu.VMEM((width, head), BF16),
            pltpu.VMEM((width, head), BF16),
            pltpu.VMEM((NC, tokens, ck), BF16),
            pltpu.VMEM((width, head), F32),
            pltpu.VMEM((width, head), BF16),
            pltpu.VMEM((NC, NY - 1, py, head), BF16),
            pltpu.VMEM((NC, NY - 1, py, head), BF16),
            pltpu.VMEM((NC, py, head), F32),
            pltpu.VMEM((NC, py, head), BF16),
            pltpu.VMEM((NC, NZ - 1, pz, head), BF16),
            pltpu.VMEM((head, head), F32),
            pltpu.VMEM((tokens, width), BF16),
            pltpu.VMEM((NX, rows, width), BF16),
            pltpu.VMEM((NX - 1, rows, width), BF16),
            pltpu.VMEM((NX - 1, rows, width), BF16),
            pltpu.VMEM((rows, width), F32),
            pltpu.VMEM((rows, width), BF16),
            pltpu.VMEM((width, head), BF16),
            dma((1 + width // 512,)),
            dma((3,)), pltpu.SemaphoreType.REGULAR((3,)),
            dma((NC, 4)), dma((NC, 4)),
            dma((NC, NX)), dma((NC, NX)),
            dma((NC, NY - 1)), dma((NC, NY - 1)),
            dma((NC,)), dma((NC,)),
            dma((NC,)), dma((NC, 4)),
            dma((NC,)), dma((NC,)),
            dma((NX,)), dma((NX,)),
            dma((NX - 1,)), dma((NX - 1,)),
            dma((NC,)),
        ],
        compiler_params=pltpu.CompilerParams(
            collective_id=0, has_side_effects=True, vmem_limit_bytes=56 * 2**20
        ),
        name="value_backward",
    )(layer_input, value_grad, value_weight, error_buffer, query_basis.T)
    input_grad, error_new, query_new = deliver(input_grad, error_new, query_new)
    return (input_grad, error_new, query_new.T)


def solution(mesh):
    return jax.shard_map(
        per_device,
        mesh=mesh,
        in_specs=(
            P(("dp", "tensor"), None),
            P("dp", "tensor"),
            P(None, "tensor"),
            P("dp", "tensor"),
            P("tensor", None),
        ),
        out_specs=(P(("dp", "tensor"), None), P("dp", "tensor"), P("tensor", None)),
        check_vma=False,
    )
```

```python
import functools

import jax
import jax.numpy as jnp
from jax import lax
from jax.experimental import pallas as pl
from jax.experimental.pallas import tpu as pltpu
from jax.sharding import PartitionSpec as P

MESH = pl.DeviceIdType.MESH
F32 = jnp.float32
BF16 = jnp.bfloat16
NY, NZ, NX, NCORE = 4, 16, 4, 2
NT = NX * NCORE
NC = 4
AHEAD = 2
FAR_FIRST = sorted(range(1, NZ), key=lambda d: -min(d, NZ - d))


def dot_rows(a, b):
    return lax.dot_general(a, b, (((0,), (0,)), ((), ())), preferred_element_type=F32)


def high(a, b, dims):
    return lax.dot_general(
        a, b, (dims, ((), ())), precision=lax.Precision.HIGHEST, preferred_element_type=F32
    )


def kernel(
    x_hbm, g_hbm, w_hbm, e_hbm, q_ref,
    ig_hbm, err_hbm, qn_ref,
    g_ref, w_ref, e_ref,
    xg, mom_ref, mean_ref, ystage, yrecv, zsum, zstage, zrecv, gram_ref,
    term, other, pair, pair_recv, home, ig_ref, err_ref,
    out_sem, load_sem, entered,
    x_send, x_recv, c_send, c_recv, ys_send, ys_recv, zs_send, zs_recv,
    zg_send, zg_recv, yg_send, yg_recv, t_send, t_recv, p_send, p_recv, own_sem,
):
    r, t = lax.axis_index("dp"), lax.axis_index("tensor")
    y, z = r // NZ, lax.rem(r, NZ)
    x, core = t // NCORE, lax.rem(t, NCORE)
    rows, width = x_hbm.shape
    tokens, head = g_hbm.shape
    rank = q_ref.shape[0]
    ck = width // NC
    py = ck // NY
    pz = py // NZ
    wide = 512

    def at_y(d):
        return (lax.rem(y + d, NY) * NZ + z, t)

    def at_z(d):
        return (y * NZ + lax.rem(z + d, NZ), t)

    def owner_x(d, c):
        return lax.rem(x + d, NX) * NCORE + c

    def at_x(d):
        return (r, owner_x(d, core))

    sibling = (r, x * NCORE + 1 - core)

    barrier = pltpu.get_barrier_semaphore()
    peers = [at_x(1), at_x(3), sibling, at_x(2), at_z(1), at_z(NZ - 1), at_y(1), at_y(3), at_y(2)]
    for peer in peers:
        pl.semaphore_signal(barrier, inc=1, device_id=peer, device_id_type=MESH)

    loads = [
        pltpu.make_async_copy(src, dst, load_sem.at[i])
        for i, (src, dst) in enumerate(((g_hbm, g_ref), (w_hbm, w_ref), (e_hbm, e_ref)))
    ]
    for cp in loads:
        cp.start()

    def block(c, owner, part=slice(None)):
        return xg.at[c, pl.ds(pl.multiple_of(owner * rows, rows), rows), part]

    own = []
    for c in range(NC):
        own.append(pltpu.make_async_copy(x_hbm.at[:, pl.ds(c * ck, ck)], block(c, t), own_sem.at[c]))
        own[c].start()
    pl.semaphore_wait(barrier, len(peers))

    sends = []

    def remote(src, dst, send, recv, device):
        cp = pltpu.make_async_remote_copy(
            src, dst, send, recv, device_id=device, device_id_type=MESH
        )
        cp.start()
        sends.append(cp)

    def spread(c):
        src = x_hbm.at[:, pl.ds(c * ck, ck)]
        remote(src, block(c, t), x_send.at[c, 0], x_recv.at[c, 0], at_x(1))
        remote(src, block(c, t), x_send.at[c, 1], x_recv.at[c, 1], at_x(3))
        remote(src, block(c, t), c_send.at[c, 0], c_recv.at[c, 0], sibling)

    def greet(i):
        if i > 0:
            pl.semaphore_wait(entered.at[i - 1], 2)
        if i < 3:
            for d in (2**i, NZ - 2**i):
                pl.semaphore_signal(entered.at[i], inc=1, device_id=at_z(d), device_id_type=MESH)

    def row_block(ref, owner):
        return ref.at[pl.ds(pl.multiple_of(owner * rows, rows), rows)]

    def head_term(i):
        if i == 0:
            loads[1].wait()

        def tile(j, carry):
            at = pl.ds(pl.multiple_of(j * wide, wide), wide)
            term[:, at] = lax.dot_general(
                g_ref[...], w_ref[at, :], (((1,), (1,)), ((), ())), preferred_element_type=F32
            ).astype(BF16)
            return carry

        quarter = width // wide // 4
        lax.fori_loop(i * quarter, (i + 1) * quarter, tile, 0)

    def term_send(i):
        for d in (1, 3, 2, 0):
            remote(
                row_block(term, owner_x(d, 1 - core)), other.at[d],
                t_send.at[d], t_recv.at[d], sibling,
            )

    def wait_bytes(ref, sem):
        pltpu.make_async_copy(ref, ref, sem).wait()

    left, right = pl.ds(0, ck // 2), pl.ds(ck // 2, ck // 2)

    def forward(c):
        for i, (d, part, to) in enumerate(((3, left, 1), (1, right, 3))):
            owner = owner_x(d, core)
            got = block(c, owner)
            wait_bytes(got, x_recv.at[c, i])
            half = block(c, owner, part)
            remote(half, half, x_send.at[c, 2 + i], x_recv.at[c, 2 + i], at_x(to))
            remote(got, got, c_send.at[c, 1 + i], c_recv.at[c, 1 + i], sibling)
        if c + AHEAD < NC:
            spread(c + AHEAD)

    def forward_far(c):
        owner = owner_x(2, core)
        wait_bytes(block(c, owner, left), x_recv.at[c, 2])
        wait_bytes(block(c, owner, right), x_recv.at[c, 3])
        got = block(c, owner)
        remote(got, got, c_send.at[c, 3], c_recv.at[c, 3], sibling)

    def moment(c):
        own[c].wait()
        if c == 0:
            loads[0].wait()
            loads[2].wait()
        for d in range(NX):
            wait_bytes(block(c, t), c_recv.at[c, d])

        for d in (1, 3, 2, 0):
            j = lax.rem(y + d, NY)
            off = pl.multiple_of(j * py, py)
            at = pl.multiple_of(c * ck + j * py, py)
            m = dot_rows(xg[c, :, pl.ds(off, py)], g_ref[...])
            m = m + e_ref[pl.ds(at, py), :].astype(F32)
            mom_ref[pl.ds(at, py), :] = m
            if d > 0:
                ystage[c, d - 1] = m.astype(BF16)
                remote(
                    ystage.at[c, d - 1], yrecv.at[c, d - 1],
                    ys_send.at[c, d - 1], ys_recv.at[c, d - 1], at_y(d),
                )

    def z_scatter(c):
        for d in range(1, NY):
            wait_bytes(yrecv.at[c, d - 1], ys_recv.at[c, d - 1])
        total = mom_ref[pl.ds(pl.multiple_of(c * ck + y * py, py), py), :]
        for d in range(1, NY):
            total = total + yrecv[c, d - 1].astype(F32)
        zsum[c] = total
        zstage[c] = total.astype(BF16)

        for d in FAR_FIRST:
            at = pl.multiple_of(lax.rem(z + d, NZ) * pz, pz)
            pltpu.make_async_remote_copy(
                zstage.at[c, pl.ds(at, pz)], zrecv.at[c, d - 1],
                zs_send.at[c], zs_recv.at[c],
                device_id=at_z(d), device_id_type=MESH,
            ).start()

    group = NZ // 4

    def z_gather(c):
        wait_bytes(zrecv.at[c], zs_recv.at[c])
        total = zsum[c, pl.ds(pl.multiple_of(z * pz, pz), pz), :]
        for d in range(1, NZ):
            total = total + zrecv[c, d - 1].astype(F32)
        at = pl.multiple_of(c * ck + y * py + z * pz, pz)
        mine = mean_ref.at[pl.ds(at, pz)]
        mine[...] = (total * (1.0 / (NY * NZ))).astype(BF16)
        for d in FAR_FIRST:
            ahead = lax.rem(z // group + 4 - lax.rem(z + d, NZ) // group, 4)
            pltpu.make_async_remote_copy(
                mine, mine, zg_send.at[c], zg_recv.at[c, ahead],
                device_id=at_z(d), device_id_type=MESH,
            ).start()

    def y_gather(c):
        for d in (0, 1, 3, 2):
            owner = lax.rem(z // group + d, 4)
            at = pl.multiple_of(c * ck + y * py + owner * group * pz, pz)
            come = group * pz - (pz if d == 0 else 0)
            wait_bytes(mean_ref.at[pl.ds(at, come)], zg_recv.at[c, d])
            mine = mean_ref.at[pl.ds(at, group * pz)]
            for dy in (2, 1, 3):
                pltpu.make_async_remote_copy(
                    mine, mine, yg_send.at[c], yg_recv.at[c],
                    device_id=at_y(dy), device_id_type=MESH,
                ).start()

    def gram(c):
        def add(rows_at, first):
            m = mean_ref[rows_at, :]
            part = dot_rows(m, m)
            gram_ref[...] = part if first else gram_ref[...] + part

        wait_bytes(mean_ref.at[pl.ds(0, (NY - 1) * py)], yg_recv.at[c])
        add(pl.ds(c * ck, ck), c == 0)

    def pair_sum(d):
        wait_bytes(other.at[d], t_recv.at[d])
        mine = row_block(term, owner_x(d, core))

        def tile(j, carry):
            at = pl.ds(pl.multiple_of(j * wide, wide), wide)
            both = mine[:, at].astype(F32) + other[d, :, at].astype(F32)
            if d == 0:
                home[:, at] = both
            else:
                pair[d - 1, :, at] = both.astype(BF16)
            return carry

        lax.fori_loop(0, width // wide, tile, 0)
        if d > 0:
            remote(pair.at[d - 1], pair_recv.at[d - 1], p_send.at[d - 1], p_recv.at[d - 1], at_x(d))

    stores = []

    def store(src, dst):
        cp = pltpu.make_async_copy(src, dst, out_sem.at[len(stores)])
        cp.start()
        stores.append(cp)

    def input_grad(c):
        for d in range(1, NX):
            wait_bytes(pair_recv.at[d - 1], p_recv.at[d - 1])

        def tile(j, carry):
            at = pl.ds(pl.multiple_of(j * wide, wide), wide)
            total = home[:, at]
            for d in range(1, NX):
                total = total + pair_recv[d - 1, :, at].astype(F32)
            ig_ref[:, at] = total.astype(BF16)
            return carry

        lax.fori_loop(0, width // wide, tile, 0)
        store(ig_ref, ig_hbm)

    def drain(c):
        while sends:
            sends.pop().wait_send()

    def drain_z(c):
        for c in range(NC):
            wait_bytes(zrecv.at[c], zs_send.at[c])

    for c in range(AHEAD):
        spread(c)
    order = [
        (greet, 0), (greet, 1), (forward, 0), (greet, 2), (forward, 1), (forward_far, 0),
        (moment, 0), (forward, 2), (forward_far, 1), (moment, 1), (forward, 3), (greet, 3),
        (forward_far, 2), (moment, 2), (z_scatter, 0), (forward_far, 3), (z_scatter, 1),
        (moment, 3), (head_term, 0), (head_term, 1), (z_scatter, 2), (head_term, 2), (head_term, 3),
        (term_send, 0), (z_scatter, 3), (pair_sum, 1), (z_gather, 0), (pair_sum, 3), (z_gather, 1),
        (pair_sum, 2), (z_gather, 2), (pair_sum, 0), (z_gather, 3), (y_gather, 0), (y_gather, 1),
        (y_gather, 2), (y_gather, 3), (gram, 0), (gram, 1), (gram, 2), (drain_z, 0), (drain, 0),
        (input_grad, 0), (gram, 3),
    ]
    for stage, c in order:
        stage(c)

    q = q_ref[...]
    prod = high(q, gram_ref[...], ((1,), (0,)))
    unit = lax.rsqrt(jnp.sum(prod * q, axis=1, keepdims=True))
    q, prod = q * unit, prod * unit
    s = high(prod, jnp.concatenate([q, jnp.zeros((head - rank, head), F32)], axis=0), ((1,), (1,)))
    row_of = lax.broadcasted_iota(jnp.int32, (rank, head), 0)
    out = jnp.zeros((rank, head), F32)
    for i in range(0, rank, 2):
        col0 = jnp.broadcast_to(s[:, i:i + 1], (rank, head))
        col1 = jnp.broadcast_to(s[:, i + 1:i + 2], (rank, head))
        a, b, d = col0[i:i + 1, :], col1[i:i + 1, :], col1[i + 1:i + 2, :]
        det = a * d - b * b
        inv = 1.0 / det
        s0, s1 = s[i:i + 1, :], s[i + 1:i + 2, :]
        p0, p1 = prod[i:i + 1, :], prod[i + 1:i + 2, :]
        first, second = row_of == i, row_of == i + 1
        out = jnp.where(first, p0 * lax.rsqrt(a), out)
        out = jnp.where(second, (p1 - (b / a) * p0) * lax.rsqrt(det / a), out)
        n0, n1 = (d * s0 - b * s1) * inv, (a * s1 - b * s0) * inv
        s = jnp.where(first, n0, jnp.where(second, n1, s - col0 * n0 - col1 * n1))
        n0, n1 = (d * p0 - b * p1) * inv, (a * p1 - b * p0) * inv
        prod = jnp.where(first, n0, jnp.where(second, n1, prod - col0 * n0 - col1 * n1))
    qn_ref[...] = out
    b = high(q, prod, ((0,), (0,)))
    b_hi = b.astype(BF16)
    b_both = jnp.concatenate([b_hi, (b - b_hi.astype(F32)).astype(BF16)], axis=0)

    for j in range(width // wide):
        at = pl.ds(j * wide, wide)
        m = mean_ref[at, :]
        approx = jnp.dot(jnp.concatenate([m, m], axis=1), b_both, preferred_element_type=F32)
        err_ref[at, :] = (mom_ref[at, :] - approx).astype(BF16)
        store(err_ref.at[at], err_hbm.at[at])

    for cp in stores:
        cp.wait()
    drain(0)
    for c in range(NC):
        wait_bytes(zrecv.at[c], zg_send.at[c])
        wait_bytes(mean_ref.at[pl.ds(0, (NY - 1) * py)], yg_send.at[c])


def deliver_kernel(
    ig_in, err_in, qn_in, ig_out, err_out, qn_out, ig_ref, err_ref, qn_ref, load_sem, store_sem
):
    n = load_sem.shape[0] - 2
    tile = err_in.shape[0] // n
    parts = [
        (err_in.at[at], err_ref.at[at], err_out.at[at])
        for at in (pl.ds(j * tile, tile) for j in range(n))
    ] + [(ig_in, ig_ref, ig_out), (qn_in, qn_ref, qn_out)]
    loads = [pltpu.make_async_copy(a, b, load_sem.at[i]) for i, (a, b, _) in enumerate(parts)]
    stores = [pltpu.make_async_copy(b, c, store_sem.at[i]) for i, (_, b, c) in enumerate(parts)]
    for cp in loads:
        cp.start()
    for load, out in zip(loads, stores):
        load.wait()
        out.start()
    for cp in stores:
        cp.wait()


def deliver(*arrays):
    hbm = pl.BlockSpec(memory_space=pl.ANY)
    n = 4
    return pl.pallas_call(
        deliver_kernel,
        out_shape=tuple(jax.ShapeDtypeStruct(a.shape, a.dtype) for a in arrays),
        in_specs=[hbm] * len(arrays),
        out_specs=(hbm,) * len(arrays),
        scratch_shapes=[pltpu.VMEM(a.shape, a.dtype) for a in arrays]
        + [pltpu.SemaphoreType.DMA((n + 2,))] * 2,
        compiler_params=pltpu.CompilerParams(vmem_limit_bytes=56 * 2**20),
        name="deliver",
    )(*arrays)


def per_device(layer_input, value_grad, value_weight, error_buffer, query_basis):
    rows, width = layer_input.shape
    tokens, head = value_grad.shape
    rank = query_basis.shape[1]
    ck = width // NC
    py = ck // NY
    pz = py // NZ
    dma = pltpu.SemaphoreType.DMA
    vmem = pl.BlockSpec(memory_space=pltpu.VMEM)
    hbm = pl.BlockSpec(memory_space=pltpu.HBM)
    input_grad, error_new, query_new = pl.pallas_call(
        kernel,
        out_shape=(
            jax.ShapeDtypeStruct((rows, width), BF16),
            jax.ShapeDtypeStruct((width, head), BF16),
            jax.ShapeDtypeStruct((rank, head), F32),
        ),
        in_specs=[hbm] * 4 + [vmem],
        out_specs=(hbm, hbm, vmem),
        scratch_shapes=[
            pltpu.VMEM((tokens, head), BF16),
            pltpu.VMEM((width, head), BF16),
            pltpu.VMEM((width, head), BF16),
            pltpu.VMEM((NC, tokens, ck), BF16),
            pltpu.VMEM((width, head), F32),
            pltpu.VMEM((width, head), BF16),
            pltpu.VMEM((NC, NY - 1, py, head), BF16),
            pltpu.VMEM((NC, NY - 1, py, head), BF16),
            pltpu.VMEM((NC, py, head), F32),
            pltpu.VMEM((NC, py, head), BF16),
            pltpu.VMEM((NC, NZ - 1, pz, head), BF16),
            pltpu.VMEM((head, head), F32),
            pltpu.VMEM((tokens, width), BF16),
            pltpu.VMEM((NX, rows, width), BF16),
            pltpu.VMEM((NX - 1, rows, width), BF16),
            pltpu.VMEM((NX - 1, rows, width), BF16),
            pltpu.VMEM((rows, width), F32),
            pltpu.VMEM((rows, width), BF16),
            pltpu.VMEM((width, head), BF16),
            dma((1 + width // 512,)),
            dma((3,)), pltpu.SemaphoreType.REGULAR((3,)),
            dma((NC, 4)), dma((NC, 4)),
            dma((NC, NX)), dma((NC, NX)),
            dma((NC, NY - 1)), dma((NC, NY - 1)),
            dma((NC,)), dma((NC,)),
            dma((NC,)), dma((NC, 4)),
            dma((NC,)), dma((NC,)),
            dma((NX,)), dma((NX,)),
            dma((NX - 1,)), dma((NX - 1,)),
            dma((NC,)),
        ],
        compiler_params=pltpu.CompilerParams(
            collective_id=0, has_side_effects=True, vmem_limit_bytes=56 * 2**20
        ),
        name="value_backward",
    )(layer_input, value_grad, value_weight, error_buffer, query_basis.T)
    input_grad, error_new, query_new = deliver(input_grad, error_new, query_new)
    return (input_grad, error_new, query_new.T)


def solution(mesh):
    return jax.shard_map(
        per_device,
        mesh=mesh,
        in_specs=(
            P(("dp", "tensor"), None),
            P("dp", "tensor"),
            P(None, "tensor"),
            P("dp", "tensor"),
            P("tensor", None),
        ),
        out_specs=(P(("dp", "tensor"), None), P("dp", "tensor"), P("tensor", None)),
        check_vma=False,
    )
```

```python
import functools

import jax
import jax.numpy as jnp
from jax import lax
from jax.experimental import pallas as pl
from jax.experimental.pallas import tpu as pltpu
from jax.sharding import PartitionSpec as P

MESH = pl.DeviceIdType.MESH
F32 = jnp.float32
BF16 = jnp.bfloat16
NY, NZ, NX, NCORE = 4, 16, 4, 2
NT = NX * NCORE
NC = 4
AHEAD = 2
FAR_FIRST = sorted(range(1, NZ), key=lambda d: -min(d, NZ - d))


def dot_rows(a, b):
    return lax.dot_general(a, b, (((0,), (0,)), ((), ())), preferred_element_type=F32)


def high(a, b, dims):
    return lax.dot_general(
        a, b, (dims, ((), ())), precision=lax.Precision.HIGHEST, preferred_element_type=F32
    )


def kernel(
    x_hbm, g_hbm, w_hbm, e_hbm, q_hbm,
    ig_hbm, err_hbm, qn_hbm,
    g_ref, w_ref, e_ref, q_ref, qn_ref,
    xg, mom_ref, mean_ref, ystage, yrecv, zsum, zstage, zrecv, gram_ref,
    term, other, pair, pair_recv, home, ig_ref, err_ref,
    out_sem, load_sem, entered,
    x_send, x_recv, c_send, c_recv, ys_send, ys_recv, zs_send, zs_recv,
    zg_send, zg_recv, yg_send, yg_recv, t_send, t_recv, p_send, p_recv, own_sem,
):
    r, t = lax.axis_index("dp"), lax.axis_index("tensor")
    y, z = r // NZ, lax.rem(r, NZ)
    x, core = t // NCORE, lax.rem(t, NCORE)
    rows, width = x_hbm.shape
    tokens, head = g_hbm.shape
    rank = q_hbm.shape[0]
    ck = width // NC
    py = ck // NY
    pz = py // NZ
    wide = 512

    def at_y(d):
        return (lax.rem(y + d, NY) * NZ + z, t)

    def at_z(d):
        return (y * NZ + lax.rem(z + d, NZ), t)

    def owner_x(d, c):
        return lax.rem(x + d, NX) * NCORE + c

    def at_x(d):
        return (r, owner_x(d, core))

    sibling = (r, x * NCORE + 1 - core)

    barrier = pltpu.get_barrier_semaphore()
    peers = [at_x(1), at_x(3), sibling, at_x(2), at_z(1), at_z(NZ - 1), at_y(1), at_y(3), at_y(2)]
    for peer in peers:
        pl.semaphore_signal(barrier, inc=1, device_id=peer, device_id_type=MESH)

    loads = [
        pltpu.make_async_copy(src, dst, load_sem.at[i])
        for i, (src, dst) in enumerate(((g_hbm, g_ref), (w_hbm, w_ref), (e_hbm, e_ref), (q_hbm, q_ref)))
    ]
    for cp in loads:
        cp.start()

    def block(c, owner, part=slice(None)):
        return xg.at[c, pl.ds(pl.multiple_of(owner * rows, rows), rows), part]

    own = []
    for c in range(NC):
        own.append(pltpu.make_async_copy(x_hbm.at[:, pl.ds(c * ck, ck)], block(c, t), own_sem.at[c]))
        own[c].start()
    pl.semaphore_wait(barrier, len(peers))

    sends = []

    def remote(src, dst, send, recv, device):
        cp = pltpu.make_async_remote_copy(
            src, dst, send, recv, device_id=device, device_id_type=MESH
        )
        cp.start()
        sends.append(cp)

    def spread(c):
        src = x_hbm.at[:, pl.ds(c * ck, ck)]
        remote(src, block(c, t), x_send.at[c, 0], x_recv.at[c, 0], at_x(1))
        remote(src, block(c, t), x_send.at[c, 1], x_recv.at[c, 1], at_x(3))
        remote(src, block(c, t), c_send.at[c, 0], c_recv.at[c, 0], sibling)

    def greet(i):
        if i > 0:
            pl.semaphore_wait(entered.at[i - 1], 2)
        if i < 3:
            for d in (2**i, NZ - 2**i):
                pl.semaphore_signal(entered.at[i], inc=1, device_id=at_z(d), device_id_type=MESH)

    def row_block(ref, owner):
        return ref.at[pl.ds(pl.multiple_of(owner * rows, rows), rows)]

    def head_term(i):
        if i == 0:
            loads[1].wait()

        def tile(j, carry):
            at = pl.ds(pl.multiple_of(j * wide, wide), wide)
            term[:, at] = lax.dot_general(
                g_ref[...], w_ref[at, :], (((1,), (1,)), ((), ())), preferred_element_type=F32
            ).astype(BF16)
            return carry

        quarter = width // wide // 4
        lax.fori_loop(i * quarter, (i + 1) * quarter, tile, 0)

    def term_send(i):
        for d in (1, 3, 2, 0):
            remote(
                row_block(term, owner_x(d, 1 - core)), other.at[d],
                t_send.at[d], t_recv.at[d], sibling,
            )

    def wait_bytes(ref, sem):
        pltpu.make_async_copy(ref, ref, sem).wait()

    left, right = pl.ds(0, ck // 2), pl.ds(ck // 2, ck // 2)

    def forward(c):
        for i, (d, part, to) in enumerate(((3, left, 1), (1, right, 3))):
            owner = owner_x(d, core)
            got = block(c, owner)
            wait_bytes(got, x_recv.at[c, i])
            half = block(c, owner, part)
            remote(half, half, x_send.at[c, 2 + i], x_recv.at[c, 2 + i], at_x(to))
            remote(got, got, c_send.at[c, 1 + i], c_recv.at[c, 1 + i], sibling)
        if c + AHEAD < NC:
            spread(c + AHEAD)

    def forward_far(c):
        owner = owner_x(2, core)
        wait_bytes(block(c, owner, left), x_recv.at[c, 2])
        wait_bytes(block(c, owner, right), x_recv.at[c, 3])
        got = block(c, owner)
        remote(got, got, c_send.at[c, 3], c_recv.at[c, 3], sibling)

    def moment(c):
        own[c].wait()
        if c == 0:
            loads[0].wait()
            loads[2].wait()
        for d in range(NX):
            wait_bytes(block(c, t), c_recv.at[c, d])

        for d in (1, 3, 2, 0):
            j = lax.rem(y + d, NY)
            off = pl.multiple_of(j * py, py)
            at = pl.multiple_of(c * ck + j * py, py)
            m = dot_rows(xg[c, :, pl.ds(off, py)], g_ref[...])
            m = m + e_ref[pl.ds(at, py), :].astype(F32)
            mom_ref[pl.ds(at, py), :] = m
            if d > 0:
                ystage[c, d - 1] = m.astype(BF16)
                remote(
                    ystage.at[c, d - 1], yrecv.at[c, d - 1],
                    ys_send.at[c, d - 1], ys_recv.at[c, d - 1], at_y(d),
                )

    def z_scatter(c):
        for d in range(1, NY):
            wait_bytes(yrecv.at[c, d - 1], ys_recv.at[c, d - 1])
        total = mom_ref[pl.ds(pl.multiple_of(c * ck + y * py, py), py), :]
        for d in range(1, NY):
            total = total + yrecv[c, d - 1].astype(F32)
        zsum[c] = total
        zstage[c] = total.astype(BF16)

        for d in FAR_FIRST:
            at = pl.multiple_of(lax.rem(z + d, NZ) * pz, pz)
            pltpu.make_async_remote_copy(
                zstage.at[c, pl.ds(at, pz)], zrecv.at[c, d - 1],
                zs_send.at[c], zs_recv.at[c],
                device_id=at_z(d), device_id_type=MESH,
            ).start()

    group = NZ // 4

    def z_gather(c):
        wait_bytes(zrecv.at[c], zs_recv.at[c])
        total = zsum[c, pl.ds(pl.multiple_of(z * pz, pz), pz), :]
        for d in range(1, NZ):
            total = total + zrecv[c, d - 1].astype(F32)
        at = pl.multiple_of(c * ck + y * py + z * pz, pz)
        mine = mean_ref.at[pl.ds(at, pz)]
        mine[...] = (total * (1.0 / (NY * NZ))).astype(BF16)
        for d in FAR_FIRST:
            ahead = lax.rem(z // group + 4 - lax.rem(z + d, NZ) // group, 4)
            pltpu.make_async_remote_copy(
                mine, mine, zg_send.at[c], zg_recv.at[c, ahead],
                device_id=at_z(d), device_id_type=MESH,
            ).start()

    def y_gather(c):
        for d in (0, 1, 3, 2):
            owner = lax.rem(z // group + d, 4)
            at = pl.multiple_of(c * ck + y * py + owner * group * pz, pz)
            come = group * pz - (pz if d == 0 else 0)
            wait_bytes(mean_ref.at[pl.ds(at, come)], zg_recv.at[c, d])
            mine = mean_ref.at[pl.ds(at, group * pz)]
            for dy in (2, 1, 3):
                pltpu.make_async_remote_copy(
                    mine, mine, yg_send.at[c], yg_recv.at[c],
                    device_id=at_y(dy), device_id_type=MESH,
                ).start()

    def gram(c):
        def add(rows_at, first):
            m = mean_ref[rows_at, :]
            part = dot_rows(m, m)
            gram_ref[...] = part if first else gram_ref[...] + part

        wait_bytes(mean_ref.at[pl.ds(0, (NY - 1) * py)], yg_recv.at[c])
        add(pl.ds(c * ck, ck), c == 0)

    def pair_sum(d):
        wait_bytes(other.at[d], t_recv.at[d])
        mine = row_block(term, owner_x(d, core))

        def tile(j, carry):
            at = pl.ds(pl.multiple_of(j * wide, wide), wide)
            both = mine[:, at].astype(F32) + other[d, :, at].astype(F32)
            if d == 0:
                home[:, at] = both
            else:
                pair[d - 1, :, at] = both.astype(BF16)
            return carry

        lax.fori_loop(0, width // wide, tile, 0)
        if d > 0:
            remote(pair.at[d - 1], pair_recv.at[d - 1], p_send.at[d - 1], p_recv.at[d - 1], at_x(d))

    stores = []

    def store(src, dst):
        cp = pltpu.make_async_copy(src, dst, out_sem.at[len(stores)])
        cp.start()
        stores.append(cp)

    def input_grad(c):
        for d in range(1, NX):
            wait_bytes(pair_recv.at[d - 1], p_recv.at[d - 1])

        def tile(j, carry):
            at = pl.ds(pl.multiple_of(j * wide, wide), wide)
            total = home[:, at]
            for d in range(1, NX):
                total = total + pair_recv[d - 1, :, at].astype(F32)
            ig_ref[:, at] = total.astype(BF16)
            return carry

        lax.fori_loop(0, width // wide, tile, 0)
        store(ig_ref, ig_hbm)

    def drain(c):
        while sends:
            sends.pop().wait_send()

    def drain_z(c):
        for c in range(NC):
            wait_bytes(zrecv.at[c], zs_send.at[c])

    for c in range(AHEAD):
        spread(c)
    order = [
        (greet, 0), (greet, 1), (forward, 0), (greet, 2), (forward, 1), (forward_far, 0),
        (moment, 0), (forward, 2), (forward_far, 1), (moment, 1), (forward, 3), (greet, 3),
        (forward_far, 2), (moment, 2), (z_scatter, 0), (forward_far, 3), (z_scatter, 1),
        (moment, 3), (head_term, 0), (head_term, 1), (z_scatter, 2), (head_term, 2), (head_term, 3),
        (term_send, 0), (z_scatter, 3), (pair_sum, 1), (z_gather, 0), (pair_sum, 3), (z_gather, 1),
        (pair_sum, 2), (z_gather, 2), (pair_sum, 0), (z_gather, 3), (y_gather, 0), (y_gather, 1),
        (y_gather, 2), (y_gather, 3), (gram, 0), (gram, 1), (gram, 2), (drain_z, 0), (drain, 0),
        (input_grad, 0), (gram, 3),
    ]
    for stage, c in order:
        stage(c)

    loads[3].wait()
    q = q_ref[...]
    prod = high(q, gram_ref[...], ((1,), (0,)))
    unit = lax.rsqrt(jnp.sum(prod * q, axis=1, keepdims=True))
    q, prod = q * unit, prod * unit
    s = high(prod, jnp.concatenate([q, jnp.zeros((head - rank, head), F32)], axis=0), ((1,), (1,)))
    row_of = lax.broadcasted_iota(jnp.int32, (rank, head), 0)
    out = jnp.zeros((rank, head), F32)
    for i in range(0, rank, 2):
        col0 = jnp.broadcast_to(s[:, i:i + 1], (rank, head))
        col1 = jnp.broadcast_to(s[:, i + 1:i + 2], (rank, head))
        a, b, d = col0[i:i + 1, :], col1[i:i + 1, :], col1[i + 1:i + 2, :]
        det = a * d - b * b
        inv = 1.0 / det
        s0, s1 = s[i:i + 1, :], s[i + 1:i + 2, :]
        p0, p1 = prod[i:i + 1, :], prod[i + 1:i + 2, :]
        first, second = row_of == i, row_of == i + 1
        out = jnp.where(first, p0 * lax.rsqrt(a), out)
        out = jnp.where(second, (p1 - (b / a) * p0) * lax.rsqrt(det / a), out)
        n0, n1 = (d * s0 - b * s1) * inv, (a * s1 - b * s0) * inv
        s = jnp.where(first, n0, jnp.where(second, n1, s - col0 * n0 - col1 * n1))
        n0, n1 = (d * p0 - b * p1) * inv, (a * p1 - b * p0) * inv
        prod = jnp.where(first, n0, jnp.where(second, n1, prod - col0 * n0 - col1 * n1))
    qn_ref[...] = out
    store(qn_ref, qn_hbm)
    b = high(q, prod, ((0,), (0,)))
    b_hi = b.astype(BF16)
    b_both = jnp.concatenate([b_hi, (b - b_hi.astype(F32)).astype(BF16)], axis=0)

    for j in range(width // wide):
        at = pl.ds(j * wide, wide)
        m = mean_ref[at, :]
        approx = jnp.dot(jnp.concatenate([m, m], axis=1), b_both, preferred_element_type=F32)
        err_ref[at, :] = (mom_ref[at, :] - approx).astype(BF16)
        store(err_ref.at[at], err_hbm.at[at])

    for cp in stores:
        cp.wait()
    drain(0)
    for c in range(NC):
        wait_bytes(zrecv.at[c], zg_send.at[c])
        wait_bytes(mean_ref.at[pl.ds(0, (NY - 1) * py)], yg_send.at[c])


def deliver_kernel(
    ig_in, err_in, qn_in, ig_out, err_out, qn_out, ig_ref, err_ref, qn_ref, load_sem, store_sem
):
    n = load_sem.shape[0] - 2
    tile = err_in.shape[0] // n
    parts = [
        (err_in.at[at], err_ref.at[at], err_out.at[at])
        for at in (pl.ds(j * tile, tile) for j in range(n))
    ] + [(ig_in, ig_ref, ig_out), (qn_in, qn_ref, qn_out)]
    loads = [pltpu.make_async_copy(a, b, load_sem.at[i]) for i, (a, b, _) in enumerate(parts)]
    stores = [pltpu.make_async_copy(b, c, store_sem.at[i]) for i, (_, b, c) in enumerate(parts)]
    for cp in loads:
        cp.start()
    for load, out in zip(loads, stores):
        load.wait()
        out.start()
    for cp in stores:
        cp.wait()


def deliver(*arrays):
    hbm = pl.BlockSpec(memory_space=pl.ANY)
    n = 4
    return pl.pallas_call(
        deliver_kernel,
        out_shape=tuple(jax.ShapeDtypeStruct(a.shape, a.dtype) for a in arrays),
        in_specs=[hbm] * len(arrays),
        out_specs=(hbm,) * len(arrays),
        scratch_shapes=[pltpu.VMEM(a.shape, a.dtype) for a in arrays]
        + [pltpu.SemaphoreType.DMA((n + 2,))] * 2,
        compiler_params=pltpu.CompilerParams(vmem_limit_bytes=56 * 2**20),
        name="deliver",
    )(*arrays)


def per_device(layer_input, value_grad, value_weight, error_buffer, query_basis):
    rows, width = layer_input.shape
    tokens, head = value_grad.shape
    rank = query_basis.shape[1]
    ck = width // NC
    py = ck // NY
    pz = py // NZ
    dma = pltpu.SemaphoreType.DMA
    hbm = pl.BlockSpec(memory_space=pltpu.HBM)
    input_grad, error_new, query_new = pl.pallas_call(
        kernel,
        out_shape=(
            jax.ShapeDtypeStruct((rows, width), BF16),
            jax.ShapeDtypeStruct((width, head), BF16),
            jax.ShapeDtypeStruct((rank, head), F32),
        ),
        in_specs=[hbm] * 5,
        out_specs=(hbm, hbm, hbm),
        scratch_shapes=[
            pltpu.VMEM((tokens, head), BF16),
            pltpu.VMEM((width, head), BF16),
            pltpu.VMEM((width, head), BF16),
            pltpu.VMEM((rank, head), F32),
            pltpu.VMEM((rank, head), F32),
            pltpu.VMEM((NC, tokens, ck), BF16),
            pltpu.VMEM((width, head), F32),
            pltpu.VMEM((width, head), BF16),
            pltpu.VMEM((NC, NY - 1, py, head), BF16),
            pltpu.VMEM((NC, NY - 1, py, head), BF16),
            pltpu.VMEM((NC, py, head), F32),
            pltpu.VMEM((NC, py, head), BF16),
            pltpu.VMEM((NC, NZ - 1, pz, head), BF16),
            pltpu.VMEM((head, head), F32),
            pltpu.VMEM((tokens, width), BF16),
            pltpu.VMEM((NX, rows, width), BF16),
            pltpu.VMEM((NX - 1, rows, width), BF16),
            pltpu.VMEM((NX - 1, rows, width), BF16),
            pltpu.VMEM((rows, width), F32),
            pltpu.VMEM((rows, width), BF16),
            pltpu.VMEM((width, head), BF16),
            dma((2 + width // 512,)),
            dma((4,)), pltpu.SemaphoreType.REGULAR((3,)),
            dma((NC, 4)), dma((NC, 4)),
            dma((NC, NX)), dma((NC, NX)),
            dma((NC, NY - 1)), dma((NC, NY - 1)),
            dma((NC,)), dma((NC,)),
            dma((NC,)), dma((NC, 4)),
            dma((NC,)), dma((NC,)),
            dma((NX,)), dma((NX,)),
            dma((NX - 1,)), dma((NX - 1,)),
            dma((NC,)),
        ],
        compiler_params=pltpu.CompilerParams(
            collective_id=0, has_side_effects=True, vmem_limit_bytes=56 * 2**20
        ),
        name="value_backward",
    )(layer_input, value_grad, value_weight, error_buffer, query_basis.T)
    input_grad, error_new, query_new = deliver(input_grad, error_new, query_new)
    return (input_grad, error_new, query_new.T)


def solution(mesh):
    return jax.shard_map(
        per_device,
        mesh=mesh,
        in_specs=(
            P(("dp", "tensor"), None),
            P("dp", "tensor"),
            P(None, "tensor"),
            P("dp", "tensor"),
            P("tensor", None),
        ),
        out_specs=(P(("dp", "tensor"), None), P("dp", "tensor"), P("tensor", None)),
        check_vma=False,
    )
```
